32 devices in a mesh: groups: 2 (over y), seq: 4 (over z), inner: 2 (over x), head: 2 (over core).
Axes of the slice: x: 2, y: 2, z: 4, core: 2. Of those that a mesh axis runs over, the one named last changes fastest.
Arguments:
- queries: bfloat16 [2048, 32, 128], P(('groups', 'seq', 'inner'), 'head'), parts along dimension 0, as said below
- keys: bfloat16 [2048, 4, 128], P(('groups', 'seq', 'inner'), 'head'), parts along dimension 0
- values: bfloat16 [2048, 4, 128], P(('groups', 'seq', 'inner'), 'head'), parts along dimension 0, may hold values from -6 to 6
- log_decay: float32 [2048, 4], P(('groups', 'seq', 'inner'), 'head'), parts along dimension 0, as said below
- gain: float32 [32, 128], P('head'), may hold values from 0.1 to 1.9
- block_list: int32 [32, 16], P(('groups', 'seq', 'inner')), parts along dimension 0, may hold values from 0 to 15, as said below
Outputs:
- attended: bfloat16 [2048, 32, 128], P(('groups', 'seq', 'inner'), 'head'), parts along dimension 0
The draws below stay inside these ranges and needn't reach their ends.
There are 2 independent parts, one for each index of `groups`. The reference program is written for one: setup_inputs(seed, part) draws one part's arguments, and reference() takes and returns one part's arrays. A program takes and returns all parts, laid end to end along the dimension named above; an argument that names none is the same for every part. Nothing has to cross between parts.
Inputs may be any that keep to these rules, and one draw needn't show every extreme that they name: Keys lie within -6 to 6; queries within -144 to 144. `log_decay`: each entry is below 0. `block_list`: entry 0 of row b is b. The sequence's pieces of 128 tokens fall into segments: piece p belongs to segment p modulo 2. Every entry of row b is a block at or before b in a piece of b's segment.
All inputs are finite; a program needn't handle non-finite values.
Results may differ from the reference program's by a relative error of at most 0.0017.
Values may be sent and summed in bfloat16 or wider, within the bound.
No kernel may reach another device: no remote copies, remote signals or barrier semaphores. Data moves between devices by JAX's collectives and lax.ppermute only.
A program may use at most 64 MiB of HBM per device.

```python
import jax
import jax.numpy as jnp
from jax import lax

HEADS = 32
KEY_VALUE_HEADS = 4
DH = 128
BLK = 64
SEL = 16
TOK_DEV = 128
SEQUENCE_TOKENS = 1024
QBLOCKS = 16
N_INNER = 2


def key_field(key):
    base = jax.random.normal(jax.random.fold_in(key, 11), (SEQUENCE_TOKENS, KEY_VALUE_HEADS, DH), jnp.float32)
    return jnp.clip(base, -6.0, 6.0)


def draw_keys(key, part):
    return key_field(key).astype(jnp.bfloat16)


def draw_queries(key, part):
    base = jax.random.normal(jax.random.fold_in(key, 12), (SEQUENCE_TOKENS, HEADS, DH), jnp.float32)
    base = jnp.clip(base, -6.0, 6.0)
    return base.astype(jnp.bfloat16)


def draw_log_decay(key, part):
    order = jax.random.permutation(jax.random.fold_in(key, 21), KEY_VALUE_HEADS)
    fast = order < (KEY_VALUE_HEADS + 1) // 2
    fast_rate = jnp.exp(jax.random.uniform(jax.random.fold_in(key, 22), (KEY_VALUE_HEADS,), jnp.float32, jnp.log(1.0 / 50.0), jnp.log(1.0 / 30.0)))
    speed_ratio = jnp.where(fast, fast_rate, 0.5 / SEQUENCE_TOKENS)
    pieces = SEQUENCE_TOKENS // TOK_DEV
    multiplier_term = jnp.exp(jax.random.uniform(jax.random.fold_in(key, 23), (pieces, KEY_VALUE_HEADS), jnp.float32, jnp.log(0.5), jnp.log(2.0)))
    multiplier_term = jnp.repeat(multiplier_term, TOK_DEV, axis=0)
    random_wobble = jax.random.uniform(jax.random.fold_in(key, 24), (SEQUENCE_TOKENS, KEY_VALUE_HEADS), jnp.float32, 0.5, 1.5)
    marked_positions = jax.random.randint(jax.random.fold_in(key, 25), (3,), 0, SEQUENCE_TOKENS)
    dropped_amounts = jnp.log(jax.random.uniform(jax.random.fold_in(key, 26), (3, KEY_VALUE_HEADS), jnp.float32, 0.5, 0.8))
    sudden_spike = jnp.zeros((SEQUENCE_TOKENS, KEY_VALUE_HEADS), jnp.float32).at[marked_positions].add(dropped_amounts)
    return -speed_ratio[None, :] * multiplier_term * random_wobble + sudden_spike


def draw_block_list(key, part):
    per_piece = TOK_DEV // BLK
    number = jnp.arange(QBLOCKS)
    piece = number // per_piece
    within = number % per_piece
    outer = piece // N_INNER
    inner_idx = piece % N_INNER
    count = outer * per_piece + within + 1
    raw = jax.random.randint(jax.random.fold_in(key, 31), (QBLOCKS, SEL), 0, 2 ** 30)
    pick = raw % count[:, None]
    chosen = (pick // per_piece * N_INNER + inner_idx[:, None]) * per_piece + pick % per_piece
    chosen = chosen.at[:, 0].set(number)
    return chosen.astype(jnp.int32)


def level_of(stream_key, extent, cuts, least, top_value):
    factor_of = 1.0
    for axis_at, shards_of in cuts:
        draws = jax.random.uniform(jax.random.fold_in(jax.random.fold_in(stream_key, 6), axis_at), (shards_of,), jnp.float32, least / len(cuts), top_value / len(cuts))
        factor_of = factor_of * jnp.repeat(jnp.exp(draws), extent[axis_at] // shards_of).reshape((-1,) + (1,) * (len(extent) - 1 - axis_at))
    return factor_of


def gaussian(own_key, shape, deviation, reach, shards=(), dtype=jnp.bfloat16):
    array = jax.random.normal(own_key, shape, jnp.float32) * deviation
    if len(shards) > 0:
        array = level_of(own_key, shape, shards, -0.22, 0.18) * array
    return jnp.clip(array, min=-reach, max=reach).astype(dtype)


def setup_inputs(seed: int = 0, part: int = 0) -> dict:
    streams_of = jax.random.split(jax.random.key(seed), 7)
    part_splits = jax.random.split(jax.random.fold_in(streams_of[6], part), 7)
    queries = draw_queries(jax.random.fold_in(jax.random.fold_in(streams_of[6], part), 71), part)
    keys = draw_keys(jax.random.fold_in(jax.random.fold_in(streams_of[6], part), 71), part)
    values = gaussian(part_splits[2], (SEQUENCE_TOKENS, KEY_VALUE_HEADS, DH), 1.0, 6.0, ((0, 8), (1, 2)))
    log_decay = draw_log_decay(jax.random.fold_in(jax.random.fold_in(streams_of[6], part), 71), part)
    gain = jnp.clip(1.0 + 0.18 * jax.random.normal(streams_of[4], (HEADS, DH), jnp.float32), 0.1, 1.9)
    block_list = draw_block_list(jax.random.fold_in(jax.random.fold_in(streams_of[6], part), 71), part)
    return dict(queries=queries, keys=keys, values=values, log_decay=log_decay, gain=gain, block_list=block_list)


HIGH = lax.Precision.HIGHEST

def linear_branch(queries, keys, values, log_decay):
    rep = HEADS // KEY_VALUE_HEADS
    count = SEQUENCE_TOKENS // TOK_DEV
    qall = queries.astype(jnp.float32).reshape(count, TOK_DEV, KEY_VALUE_HEADS, rep, DH)
    kall = keys.astype(jnp.float32).reshape(count, TOK_DEV, KEY_VALUE_HEADS, DH)
    vall = values.astype(jnp.float32).reshape(count, TOK_DEV, KEY_VALUE_HEADS, DH)
    dall = log_decay.reshape(count, TOK_DEV, KEY_VALUE_HEADS)
    causal = jnp.arange(TOK_DEV)[:, None] >= jnp.arange(TOK_DEV)[None, :]

    def step(state, piece):
        qf, kf, vf, dec = piece
        cum = jnp.cumsum(dec, axis=0)
        total = cum[-1]
        scores = jnp.einsum('tkrd,skd->krts', qf, kf, precision=HIGH)
        diff = cum.T[:, :, None] - cum.T[:, None, :]
        weight = jnp.where(causal[None], jnp.exp(jnp.minimum(diff, 0.0)), 0.0)
        intra = jnp.einsum('krts,skd->tkrd', scores * weight[:, None], vf, precision=HIGH)
        inter = jnp.exp(cum)[:, :, None, None] * jnp.einsum('tkrd,kde->tkre', qf, state, precision=HIGH)
        tail = jnp.exp(total[None, :] - cum)
        own_state = jnp.einsum('skd,ske->kde', kf * tail[:, :, None], vf, precision=HIGH)
        new_state = jnp.exp(total)[:, None, None] * state + own_state
        return (new_state, (intra + inter).reshape(TOK_DEV, HEADS, DH))
    start = jnp.zeros((KEY_VALUE_HEADS, DH, DH), jnp.float32)
    final_state, pieces = lax.scan(step, start, (qall, kall, vall, dall))
    return pieces.reshape(SEQUENCE_TOKENS, HEADS, DH)

def sparse_branch(queries, keys, values, block_list):
    rep = HEADS // KEY_VALUE_HEADS
    kblocks = keys.astype(jnp.float32).reshape(QBLOCKS, BLK, KEY_VALUE_HEADS, DH)
    vblocks = values.astype(jnp.float32).reshape(QBLOCKS, BLK, KEY_VALUE_HEADS, DH)
    qblocks = queries.astype(jnp.float32).reshape(QBLOCKS, BLK, KEY_VALUE_HEADS, rep, DH)
    lower = jnp.arange(SEL)[None, :] < jnp.arange(SEL)[:, None]

    def one_block(args):
        qblk, sel, number = args
        pk = kblocks[sel]
        pv = vblocks[sel]
        repeat = jnp.any((sel[:, None] == sel[None, :]) & lower, axis=1)
        keep = jnp.logical_not(repeat)
        qpos = number * BLK + jnp.arange(BLK)
        kpos = sel[:, None] * BLK + jnp.arange(BLK)[None, :]
        valid = keep[None, :, None] & (kpos[None] <= qpos[:, None, None])
        score = jnp.einsum('qkrd,jukd->krqju', qblk, pk, precision=HIGH) * DH ** (-0.5)
        score = jnp.where(valid[None, None], score, -1e+30)
        top = lax.optimization_barrier(jnp.max(score, axis=(3, 4), keepdims=True))
        expo = jnp.where(valid[None, None], jnp.exp(score - top), 0.0)
        denom = lax.optimization_barrier(jnp.sum(expo, axis=(3, 4)))
        weights = expo.astype(jnp.bfloat16).astype(jnp.float32)
        out = jnp.einsum('krqju,jukd->qkrd', weights, pv, precision=HIGH)
        return out / jnp.transpose(denom, (2, 0, 1))[:, :, :, None]
    numbers = jnp.arange(QBLOCKS).astype(jnp.int32)
    outs = lax.map(one_block, (qblocks, block_list, numbers))
    return outs.reshape(SEQUENCE_TOKENS, HEADS, DH)

def reference(queries, keys, values, log_decay, gain, block_list):
    linear = linear_branch(queries, keys, values, log_decay)
    normed = linear * lax.rsqrt(lax.optimization_barrier(jnp.mean(linear * linear, axis=-1, keepdims=True)) + 1e-06) * gain[None]
    sparse = sparse_branch(queries, keys, values, block_list)
    return (normed + sparse).astype(jnp.bfloat16)
```

```python
import functools

import jax
import jax.numpy as jnp
from jax import lax
from jax.experimental import pallas as pl
from jax.experimental.pallas import tpu as pltpu
from jax.sharding import PartitionSpec as P

BLK = 64
EXTRA = 16
HIGH = lax.Precision.HIGHEST
F32 = jnp.float32
BF16 = jnp.bfloat16
NT = (((1,), (1,)), ((), ()))
TN = (((0,), (0,)), ((), ()))
NEG = -1e30
VMEM = pl.BlockSpec(memory_space=pltpu.VMEM)
SMEM = pl.BlockSpec(memory_space=pltpu.SMEM)
PARAMS = pltpu.CompilerParams(vmem_limit_bytes=48 * 2**20)


def iota(shape, dim):
    return lax.broadcasted_iota(jnp.int32, shape, dim)


def mm(a, b, dims=(((1,), (0,)), ((), ())), precision=None):
    return lax.dot_general(a, b, dims, preferred_element_type=F32, precision=precision)


def halves(x):
    hi = x.astype(BF16)
    return hi, (x - hi.astype(F32)).astype(BF16)


def pack_kernel(kv, keys, values, decay, out, even):
    tokens = keys.shape[0] // kv
    for n, ref in enumerate((keys, values)):
        even[...] = ref[...].astype(F32)
        for g in range(kv):
            at = (n * kv + g) * tokens
            out[at : at + tokens, :] = even[pl.ds(g, tokens, stride=kv), :].astype(BF16)
    left = jnp.maximum(decay[...], NEG)
    parts = []
    for _ in range(3):
        parts.append(left.astype(BF16).astype(F32))
        left = left - parts[-1]
    rest = jnp.zeros((EXTRA - 3 * kv, tokens), F32)
    out[2 * kv * tokens :, :] = jnp.concatenate([*parts, rest], axis=0).astype(BF16)


def decays(piece, kv):
    rows = piece[piece.shape[0] - EXTRA :, :].astype(F32)
    return rows[:kv] + rows[kv : 2 * kv] + rows[2 * kv : 3 * kv]


def local_kernel(kv, queries, piece, q_out, lin_out):
    tokens, heads, width = queries.shape
    rep = heads // kv
    rows = tokens * rep
    qf = queries[...].astype(F32)
    dec = decays(piece, kv)
    upto = (iota((rows, tokens), 1) <= iota((rows, tokens), 0) // rep).astype(F32)
    dec8 = jnp.concatenate([dec, jnp.zeros((8 - kv, tokens), F32)], axis=0)
    ahead = (iota((tokens, tokens), 0) <= iota((tokens, tokens), 1)).astype(F32)
    cum_row = mm(dec8, ahead, precision=HIGH)
    cum_col = mm(upto, dec8, NT, precision=HIGH)
    for g in range(kv):
        q = qf[:, g * rep : (g + 1) * rep, :].reshape(rows, width).astype(BF16)
        q_out[g] = q
        k = piece[g * tokens : (g + 1) * tokens, :]
        v = piece[(kv + g) * tokens : (kv + g + 1) * tokens, :]
        diff = cum_col[:, g : g + 1] - cum_row[g : g + 1, :]
        weight = jnp.where(upto > 0, jnp.exp(jnp.minimum(diff, 0.0)), 0.0)
        hi, lo = halves(mm(q, k, NT) * weight)
        lin_out[g] = mm(hi, v) + mm(lo, v)


def sparse_kernel(kv, slots, ids, n_mine, queries, blocks, *refs):
    pieces, out, scores = refs[:n_mine], refs[-2], refs[-1]
    _, rows, width = queries.shape
    per = blocks.shape[0]
    tokens = per * BLK
    rep = rows // tokens
    here, number = ids()
    factor = width**-0.5 * 1.4426950408889634
    part = rows // per

    def piece_of(i):
        return pieces[i] if n_mine > 1 else pieces[0].at[i]

    lane = iota((1, tokens), 1)
    for b in range(per):
        biases = []
        for i in range(slots):
            block = number(i) * per + lane // BLK
            listed = block == blocks[b, 0]
            for j in range(1, blocks.shape[1]):
                listed = jnp.logical_or(listed, block == blocks[b, j])
            biases.append(jnp.where(listed, 0.0, NEG))
        row = b * BLK + iota((part, tokens), 0) // rep
        position = here * tokens + row
        for g in range(kv):
            q = queries[g, b * part : (b + 1) * part, :]
            top = None
            for i in range(slots):
                k = piece_of(i)[g * tokens : (g + 1) * tokens, :]
                s = mm(q, k, NT) + biases[i]
                if n_mine == 1 or i == 0:
                    s = jnp.where(number(i) * tokens + iota((part, tokens), 1) <= position, s, NEG)
                scores[:, i * tokens : (i + 1) * tokens] = s
                top = s if top is None else jnp.maximum(top, s)
            top = jnp.max(top, axis=1, keepdims=True)
            total, acc = None, None
            for i in range(slots):
                v = piece_of(i)[(kv + g) * tokens : (kv + g + 1) * tokens, :]
                e = jnp.exp2((scores[:, i * tokens : (i + 1) * tokens] - top) * factor)
                o = mm(e.astype(BF16), v)
                total = e if total is None else total + e
                acc = o if acc is None else acc + o
            denom = jnp.sum(total, axis=1, keepdims=True)
            out[g, b * part : (b + 1) * part, :] = acc / denom


def final_kernel(kv, slots, distance, n_mine, queries, lin, sparse, gain, own, *refs):
    pieces, out = refs[:n_mine], refs[-1]
    _, rows, width = queries.shape
    tokens, heads, _ = out.shape
    rep = heads // kv
    after = (iota((tokens, tokens), 1) > iota((tokens, tokens), 0)).astype(F32)

    def terms(piece, dec, shift, keep, state):
        suffix = mm(after, dec, NT, precision=HIGH)
        result = []
        for g in range(kv):
            w = jnp.exp(jnp.minimum(suffix[:, g : g + 1] + shift[g], 0.0))
            w = jnp.where(keep, w, 0.0)
            k = piece[g * tokens : (g + 1) * tokens, :]
            v = piece[(kv + g) * tokens : (kv + g + 1) * tokens, :].astype(F32) * w
            hi, lo = halves(v)
            result.append(state[g] + mm(k, hi, TN) + mm(k, lo, TN))
        return result

    def padded(piece):
        return jnp.concatenate([decays(piece, kv), jnp.zeros((8 - kv, tokens), F32)], axis=0)

    state = [jnp.zeros((width, width), F32) for _ in range(kv)]
    if n_mine > 1:
        decs = [padded(p) for p in pieces]
        totals = [jnp.sum(d, axis=1, keepdims=True) for d in decs]
        where = [distance(i) for i in range(slots)]
        for i in range(slots):
            shift = jnp.zeros((8, 1), F32)
            for j in range(slots):
                if j != i:
                    between = jnp.logical_and(where[j] >= 1, where[j] < where[i])
                    shift = shift + jnp.where(between, totals[j], 0.0)
            keep = distance(i, True)
            shifts = [shift[g : g + 1, :] for g in range(kv)]
            state = terms(pieces[i], decs[i], shifts, keep, state)
    else:

        def turn(n, carry):
            shift, state = carry
            at, keep = distance(n)
            piece = pieces[0].at[at]
            dec = padded(piece)
            state = terms(piece, dec, [shift[g : g + 1, :] for g in range(kv)], keep, state)
            total = jnp.sum(dec, axis=1, keepdims=True)
            return shift + jnp.where(keep, total, 0.0), tuple(state)

        _, state = lax.fori_loop(0, slots, turn, (jnp.zeros((8, 1), F32), tuple(state)))
    upto = (iota((rows, tokens), 1) <= iota((rows, tokens), 0) // rep).astype(F32)
    cum = mm(upto, padded(own), NT, precision=HIGH)
    both = []
    for g in range(kv):
        q = queries[g]
        hi, lo = halves(state[g])
        inter = mm(q, hi) + mm(q, lo)
        linear = lin[g] + jnp.exp(cum[:, g : g + 1]) * inter
        mean = jnp.mean(linear * linear, axis=1, keepdims=True)
        normed = (linear * lax.rsqrt(mean + 1e-06)).reshape(tokens, rep, width)
        normed = normed * gain[g * rep : (g + 1) * rep, :][None]
        both.append(normed + sparse[g].reshape(tokens, rep, width))
    out[...] = jnp.concatenate(both, axis=1).astype(BF16)


def shards(queries, keys, values, log_decay, gain, block_list):
    tokens, heads, width = queries.shape
    kv = keys.shape[1]
    rep = heads // kv
    rows = tokens * rep
    n_seq, n_inner = lax.axis_size("seq"), lax.axis_size("inner")
    shape = jax.ShapeDtypeStruct
    piece = pl.pallas_call(
        functools.partial(pack_kernel, kv),
        out_shape=shape((2 * kv * tokens + EXTRA, width), BF16),
        in_specs=[VMEM] * 3,
        out_specs=VMEM,
        scratch_shapes=[pltpu.VMEM((tokens * kv, width), F32)],
        compiler_params=PARAMS,
    )(keys.reshape(-1, width), values.reshape(-1, width), log_decay.T)
    q, lin = pl.pallas_call(
        functools.partial(local_kernel, kv),
        out_shape=(shape((kv, rows, width), BF16), shape((kv, rows, width), F32)),
        in_specs=[VMEM] * 2,
        out_specs=(VMEM, VMEM),
        compiler_params=PARAMS,
    )(queries, piece)

    few = n_seq == 4 and n_inner == 2
    if few:
        def forward(x, s):
            return lax.ppermute(x, "seq", [(i, i + s) for i in range(n_seq - s)])

        moved = {s: forward(piece, s) for s in range(n_seq - 1, 0, -1)}
        column = [piece, *(moved[s] for s in range(1, n_seq))]
        other = [lax.ppermute(x, "inner", [(0, 1), (1, 0)]) for x in column]

        def ids():
            z, x = lax.axis_index("seq"), lax.axis_index("inner")
            return z * n_inner + x, lambda i: (z - i) * n_inner + x

        def distance(i, keep=False):
            z, x = lax.axis_index("seq"), lax.axis_index("inner")
            if i < n_seq - 1:
                back, far = i + 1, (i + 1) * n_inner
            else:
                back = i - (n_seq - 1)
                far = back * n_inner + jnp.where(x == 0, -1, 1)
            return jnp.logical_and(far >= 1, back <= z) if keep else far

        sparse_in, final_in = column, column[1:] + other
        slots, n_all = n_seq, 2 * n_seq - 1
    else:
        column = lax.all_gather(piece, "seq")
        everything = lax.all_gather(column, "inner").reshape(n_inner * n_seq, *piece.shape)

        def ids():
            z, x = lax.axis_index("seq"), lax.axis_index("inner")
            return z * n_inner + x, lambda i: i * n_inner + x

        def distance(n):
            here = lax.axis_index("seq") * n_inner + lax.axis_index("inner")
            p = n_seq * n_inner - 1 - n
            return lax.rem(p, n_inner) * n_seq + lax.div(p, n_inner), p < here

        sparse_in, final_in = [column], [everything]
        slots, n_all = n_seq, n_seq * n_inner

    per = tokens // BLK
    sparse = pl.pallas_call(
        functools.partial(sparse_kernel, kv, slots, ids, len(sparse_in)),
        out_shape=shape((kv, rows, width), F32),
        in_specs=[VMEM, SMEM] + [VMEM] * len(sparse_in),
        out_specs=VMEM,
        scratch_shapes=[pltpu.VMEM((rows // per, slots * tokens), F32)],
        compiler_params=PARAMS,
    )(q, block_list, *sparse_in)
    return pl.pallas_call(
        functools.partial(final_kernel, kv, n_all, distance, len(final_in)),
        out_shape=shape((tokens, heads, width), BF16),
        in_specs=[VMEM] * (5 + len(final_in)),
        out_specs=VMEM,
        compiler_params=PARAMS,
    )(q, lin, sparse, gain, piece, *final_in)


def solution(mesh):
    tokens = P(("groups", "seq", "inner"), "head", None)
    return jax.shard_map(
        shards,
        mesh=mesh,
        in_specs=(
            tokens,
            tokens,
            tokens,
            P(("groups", "seq", "inner"), "head"),
            P("head", None),
            P(("groups", "seq", "inner"), None),
        ),
        out_specs=tokens,
        check_vma=False,
    )
```

```python
import functools

import jax
import jax.numpy as jnp
from jax import lax
from jax.experimental import pallas as pl
from jax.experimental.pallas import tpu as pltpu
from jax.sharding import PartitionSpec as P

BLK = 64
EXTRA = 16
F32 = jnp.float32
BF16 = jnp.bfloat16
NT = (((1,), (1,)), ((), ()))
TN = (((0,), (0,)), ((), ()))
NEG = -1e30
NEVER = 1 << 20
VMEM = pl.BlockSpec(memory_space=pltpu.VMEM)
HBM = pl.BlockSpec(memory_space=pltpu.HBM)
SMEM = pl.BlockSpec(memory_space=pltpu.SMEM)
PARAMS = pltpu.CompilerParams(vmem_limit_bytes=48 * 2**20)


def iota(shape, dim):
    return lax.broadcasted_iota(jnp.int32, shape, dim)


def mm(a, b, dims=(((1,), (0,)), ((), ()))):
    return lax.dot_general(a, b, dims, preferred_element_type=F32)


def halves(x):
    hi = x.astype(BF16)
    return hi, (x - hi.astype(F32)).astype(BF16)


def pack_kernel(kv, keys, values, decay, out, kv_in, decay_in, even, sems):
    tokens = keys.shape[0] // kv
    copies = [
        pltpu.make_async_copy(keys, kv_in.at[0], sems.at[0]),
        pltpu.make_async_copy(values, kv_in.at[1], sems.at[1]),
        pltpu.make_async_copy(decay, decay_in, sems.at[2]),
    ]
    for c in copies:
        c.start()
    for n in range(2):
        copies[n].wait()
        even[...] = kv_in[n].astype(F32)
        for g in range(kv):
            at = (n * kv + g) * tokens
            out[at : at + tokens, :] = even[pl.ds(g, tokens, stride=kv), :].astype(BF16)
    copies[2].wait()
    left = jnp.maximum(decay_in[...], NEG)
    parts = []
    for _ in range(3):
        parts.append(left.astype(BF16).astype(F32))
        left = left - parts[-1]
    rest = jnp.zeros((EXTRA - 3 * kv, tokens), F32)
    out[2 * kv * tokens :, :] = jnp.concatenate([*parts, rest], axis=0).astype(BF16)


def parts_of(piece, kv):
    rows = piece[piece.shape[0] - EXTRA :, :].astype(F32)
    rest = jnp.zeros((8 - kv, rows.shape[1]), F32)
    return [jnp.concatenate([rows[n * kv : (n + 1) * kv], rest], axis=0) for n in range(3)]


def block_biases(number, per, blocks, b, tokens):
    block = number * per + iota((1, tokens), 1) // BLK
    listed = block == blocks[b, 0]
    for j in range(1, blocks.shape[1]):
        listed = jnp.logical_or(listed, block == blocks[b, j])
    return jnp.where(listed, 0.0, NEG)


def local_kernel(kv, numbers, queries, piece, blocks, gain, q_out, lin_out, grown_out, bias_out, gain_out, q_in, sems):
    copy = pltpu.make_async_copy(queries, q_in, sems.at[0])
    copy.start()
    gain_copy = pltpu.make_async_copy(gain, gain_out, sems.at[1])
    gain_copy.start()
    tokens, heads, width = queries.shape
    rep = heads // kv
    rows = tokens * rep
    per = blocks.shape[0]
    parts = [p.astype(BF16) for p in parts_of(piece, kv)]
    upto = iota((rows, tokens), 1) <= iota((rows, tokens), 0) // rep
    ones = jnp.where(upto, 1.0, 0.0).astype(BF16)
    ahead = jnp.where(iota((tokens, tokens), 0) <= iota((tokens, tokens), 1), 1.0, 0.0).astype(BF16)
    cum_row = mm(parts[0], ahead) + mm(parts[1], ahead) + mm(parts[2], ahead)
    cum_col = mm(ones, parts[0], NT) + mm(ones, parts[1], NT) + mm(ones, parts[2], NT)
    if numbers is not None:
        rows_of = [block_biases(n, per, blocks, b, tokens) for b in range(per) for n in numbers()]
        for r, row in enumerate(rows_of):
            bias_out[r : r + 1, :] = row
    copy.wait()
    qf = q_in[...].astype(F32)
    for g in range(kv):
        q = qf[:, g * rep : (g + 1) * rep, :].reshape(rows, width).astype(BF16)
        q_out[g] = q
        k = piece[g * tokens : (g + 1) * tokens, :]
        v = piece[(kv + g) * tokens : (kv + g + 1) * tokens, :]
        cum = jnp.broadcast_to(cum_col[:, g : g + 1], (rows, tokens))
        grown_out[g] = jnp.exp(cum)
        weight = jnp.where(upto, jnp.exp(jnp.minimum(cum - cum_row[g : g + 1, :], 0.0)), 0.0)
        hi, lo = halves(mm(q, k, NT) * weight)
        lin_out[g] = mm(hi, v) + mm(lo, v)
    gain_copy.wait()


def attend(kv, b, per, queries, pieces, biases, own, scores, out):
    _, rows, width = queries.shape
    part = rows // per
    factor = width**-0.5 * 1.4426950408889634
    tokens = scores.shape[1] // len(pieces)
    for g in range(kv):
        q = queries[g, b * part : (b + 1) * part, :]
        top = None
        for i, piece in enumerate(pieces):
            s = mm(q, piece[g * tokens : (g + 1) * tokens, :], NT) + biases[i]
            mask = own(i, (part, tokens))
            if mask is not None:
                s = jnp.where(mask, s, NEG)
            scores[:, i * tokens : (i + 1) * tokens] = s
            top = s if top is None else jnp.maximum(top, s)
        top = jnp.max(top, axis=1, keepdims=True)
        total, acc = None, None
        for i, piece in enumerate(pieces):
            e = jnp.exp2((scores[:, i * tokens : (i + 1) * tokens] - top) * factor)
            o = mm(e.astype(BF16), piece[(kv + g) * tokens : (kv + g + 1) * tokens, :])
            total = e if total is None else total + e
            acc = o if acc is None else acc + o
        out[g, b * part : (b + 1) * part, :] = acc / jnp.sum(total, axis=1, keepdims=True)


def suffixes(parts, tokens):
    after = jnp.where(iota((tokens, tokens), 1) > iota((tokens, tokens), 0), 1.0, 0.0).astype(BF16)
    hi, mid, lo = (p.astype(BF16) for p in parts)
    return mm(after, hi, NT) + mm(after, mid, NT) + mm(after, lo, NT)


def totals(parts):
    return jnp.sum(parts[0] + parts[1] + parts[2], axis=1, keepdims=True)


def own_states(kv, piece, suffix, shift):
    tokens = suffix.shape[0]
    result = []
    for g in range(kv):
        w = jnp.exp(jnp.minimum(suffix[:, g : g + 1] + shift[g], 0.0))
        k = piece[g * tokens : (g + 1) * tokens, :]
        hi, lo = halves(piece[(kv + g) * tokens : (kv + g + 1) * tokens, :].astype(F32) * w)
        result.append(mm(k, hi, TN) + mm(k, lo, TN))
    return result


def finish(kv, queries, lin, grown, sparse, gain, state, out):
    _, rows, width = queries.shape
    tokens, heads, _ = out.shape
    rep = heads // kv
    both = []
    for g in range(kv):
        q = queries[g]
        hi, lo = halves(state[g])
        linear = lin[g] + grown[g] * (mm(q, hi) + mm(q, lo))
        mean = jnp.mean(linear * linear, axis=1, keepdims=True)
        normed = (linear * lax.rsqrt(mean + 1e-06)).reshape(tokens, rep, width)
        normed = normed * gain[g * rep : (g + 1) * rep, :][None]
        both.append(normed + sparse[g].reshape(tokens, rep, width))
    out[...] = jnp.concatenate(both, axis=1).astype(BF16)


def column_kernel(kv, slots, ids, queries, blocks, column, out, scores):
    per = blocks.shape[0]
    tokens = per * BLK
    rep = queries.shape[1] // tokens
    here, number = ids()
    for b in range(per):

        def own(i, shape):
            position = here * tokens + b * BLK + iota(shape, 0) // rep
            return number(i) * tokens + iota(shape, 1) <= position

        biases = [block_biases(number(i), per, blocks, b, tokens) for i in range(slots)]
        attend(kv, b, per, queries, [column.at[i] for i in range(slots)], biases, own, scores, out)


def final_kernel(kv, slots, place, queries, lin, grown, sparse, gain, everything, out):
    tokens = out.shape[0]
    width = queries.shape[2]

    def turn(n, carry):
        shift, state = carry
        at, keep = place(n)
        piece = everything.at[at]
        parts = parts_of(piece, kv)
        shifts = [shift[g : g + 1, :] for g in range(kv)]
        more = own_states(kv, piece, suffixes(parts, tokens), shifts)
        state = tuple(s + jnp.where(keep, m, 0.0) for s, m in zip(state, more))
        return shift + jnp.where(keep, totals(parts), 0.0), state

    zero = tuple(jnp.zeros((width, width), F32) for _ in range(kv))
    _, state = lax.fori_loop(0, slots, turn, (jnp.zeros((8, 1), F32), zero))
    finish(kv, queries, lin, grown, sparse, gain, state, out)


def shift_of(i, sums, far):
    shift = jnp.zeros((8, 1), F32)
    for j, total in enumerate(sums):
        if j != i:
            shift = shift + jnp.where(far[j] < far[-1 if i is None else i], total, 0.0)
    return shift


def sparse_kernel(kv, n_column, per, distance, queries, biases, *refs):
    *pieces, out, states, factor, scores = refs
    column = pieces[:n_column]
    tokens = per * BLK
    rep = queries.shape[1] // tokens
    far = distance()
    parts = [parts_of(p, kv) for p in pieces[1:]]
    suffix = suffixes([jnp.concatenate(p, axis=0) for p in zip(*parts)], tokens)
    sums = [totals(p) for p in parts]
    near, beyond = [0.0] * kv, [0.0] * kv
    for i, piece in enumerate(pieces[1:]):
        shift = shift_of(i, sums, far)
        more = own_states(kv, piece, suffix[:, 8 * i : 8 * i + 8], [shift[g : g + 1, :] for g in range(kv)])
        closer = far[i] < far[-1]
        behind = jnp.logical_and(far[i] > far[-1], far[i] < NEVER)
        for g in range(kv):
            near[g] = near[g] + jnp.where(closer, more[g], 0.0)
            beyond[g] = beyond[g] + jnp.where(behind, more[g], 0.0)
    for g in range(kv):
        states[g], states[kv + g] = near[g], beyond[g]
    factor[...] = jnp.broadcast_to(jnp.exp(shift_of(None, sums, far)), factor.shape)
    for b in range(per):

        def own(i, shape):
            return iota(shape, 1) <= b * BLK + iota(shape, 0) // rep if i == 0 else None

        rows = [biases[b * n_column + i : b * n_column + i + 1, :] for i in range(n_column)]
        attend(kv, b, per, queries, column, rows, own, scores, out)


def last_kernel(kv, distance, queries, lin, grown, sparse, gain, states, factor, last, out):
    parts = parts_of(last, kv)
    total = jnp.exp(totals(parts))
    keep = distance()[-1] < NEVER
    more = own_states(kv, last, suffixes(parts, out.shape[0]), [0.0] * kv)
    state = []
    for g in range(kv):
        mine = jnp.where(keep, factor[g : g + 1, :] * more[g], 0.0)
        state.append(states[g] + jnp.where(keep, total[g : g + 1, :] * states[kv + g], 0.0) + mine)
    finish(kv, queries, lin, grown, sparse, gain, state, out)


def where_am_i():
    return lax.axis_index("seq"), lax.axis_index("inner")


def pick(table, at):
    value = jnp.int32(table[0])
    for n in range(1, len(table)):
        value = jnp.where(at == n, table[n], value)
    return value


def in_hbm(x):
    return pltpu.with_memory_space_constraint(x, pltpu.HBM)


def shards(queries, keys, values, log_decay, gain, block_list):
    tokens, heads, width = queries.shape
    kv = keys.shape[1]
    rows = tokens * (heads // kv)
    per = tokens // BLK
    n_seq, n_inner = lax.axis_size("seq"), lax.axis_size("inner")
    shape = jax.ShapeDtypeStruct

    def call(kernel, out_shape, in_specs, scratch, *args, cost=None):
        one = not isinstance(out_shape, tuple)
        return pl.pallas_call(
            kernel,
            out_shape=out_shape,
            in_specs=in_specs,
            out_specs=VMEM if one else tuple(VMEM for _ in out_shape),
            scratch_shapes=scratch,
            compiler_params=PARAMS,
            cost_estimate=cost,
        )(*args)

    piece = call(
        functools.partial(pack_kernel, kv),
        shape((2 * kv * tokens + EXTRA, width), BF16),
        [HBM] * 3,
        [
            pltpu.VMEM((2, kv * tokens, width), BF16),
            pltpu.VMEM((kv, tokens), F32),
            pltpu.VMEM((kv * tokens, width), F32),
            pltpu.SemaphoreType.DMA((3,)),
        ],
        in_hbm(keys.reshape(-1, width)),
        in_hbm(values.reshape(-1, width)),
        in_hbm(log_decay.T),
    )
    few = n_seq == 4 and n_inner == 2

    def numbers():
        z, x = where_am_i()
        found = [z * n_inner + x]
        for table in held:
            other = pick(table, z)
            found.append(jnp.where(other < z, other * n_inner + x, -1))
        return found

    def distance():
        z, x = where_am_i()
        mine, theirs = [], [jnp.where(x == 1, 1, NEVER)]
        for table in held:
            other = pick(table, z)
            mine.append(jnp.where(other < z, (z - other) * n_inner, NEVER))
            theirs.append(jnp.where(other < z, (z - other) * n_inner + jnp.where(x == 1, 1, -1), NEVER))
        return mine + theirs

    if few:
        first, second, third = (
            [(0, 2), (2, 3), (1, 1), (3, 0)],
            [(0, 1), (1, 3), (3, 2), (2, 0)],
            [(1, 2), (2, 3), (0, 0), (3, 1)],
        )
        came = [{b: a for a, b in pairs} for pairs in (first, second, third)]
        held = [[came[0][i] for i in range(4)], [came[1][i] for i in range(4)], [came[0][came[2][i]] for i in range(4)]]

    q, lin, grown, biases, gain = call(
        functools.partial(local_kernel, kv, numbers if few else None),
        (
            shape((kv, rows, width), BF16),
            shape((kv, rows, width), F32),
            shape((kv, rows, tokens), F32),
            shape((8, tokens), F32),
            shape(gain.shape, F32),
        ),
        [HBM, VMEM, SMEM, HBM],
        [pltpu.VMEM(queries.shape, BF16), pltpu.SemaphoreType.DMA((2,))],
        in_hbm(queries),
        piece,
        block_list,
        in_hbm(gain),
        cost=pl.CostEstimate(flops=4 * 10**9, bytes_accessed=4 * 10**6, transcendentals=10**6),
    )
    if few:

        def swap(x):
            return lax.ppermute(x, "inner", [(0, 1), (1, 0)])

        theirs = swap(piece)
        got1 = lax.ppermute(piece, "seq", first)
        got2 = lax.ppermute(piece, "seq", second)
        got1, q, theirs = lax.optimization_barrier((got1, q, theirs))
        got3 = lax.ppermute(got1, "seq", third)
        column = [piece, got1, got2, got3]
        other = [theirs, *(swap(x) for x in column[1:])]

    out_shape = shape((tokens, heads, width), BF16)
    if few:
        sparse, states, factor = call(
            functools.partial(sparse_kernel, kv, n_seq, per, distance),
            (shape((kv, rows, width), F32), shape((2 * kv, width, width), F32), shape((8, width), F32)),
            [VMEM] * (2 + 2 * n_seq - 1),
            [pltpu.VMEM((rows // per, n_seq * tokens), F32)],
            q,
            biases,
            *column,
            *other[:-1],
        )
        return call(
            functools.partial(last_kernel, kv, distance),
            out_shape,
            [VMEM] * 8,
            [],
            q,
            lin,
            grown,
            sparse,
            gain,
            states,
            factor,
            other[-1],
        )

    column = lax.all_gather(piece, "seq")
    everything = lax.all_gather(column, "inner").reshape(n_inner * n_seq, *piece.shape)

    def ids():
        z, x = where_am_i()
        return z * n_inner + x, lambda i: i * n_inner + x

    def place(n):
        z, x = where_am_i()
        p = n_seq * n_inner - 1 - n
        return lax.rem(p, n_inner) * n_seq + lax.div(p, n_inner), p < z * n_inner + x

    sparse = call(
        functools.partial(column_kernel, kv, n_seq, ids),
        shape((kv, rows, width), F32),
        [VMEM, SMEM, VMEM],
        [pltpu.VMEM((rows // per, n_seq * tokens), F32)],
        q,
        block_list,
        column,
    )
    return call(
        functools.partial(final_kernel, kv, n_seq * n_inner, place),
        out_shape,
        [VMEM] * 6,
        [],
        q,
        lin,
        grown,
        sparse,
        gain,
        everything,
    )


def solution(mesh):
    tokens = P(("groups", "seq", "inner"), "head", None)
    return jax.shard_map(
        shards,
        mesh=mesh,
        in_specs=(
            tokens,
            tokens,
            tokens,
            P(("groups", "seq", "inner"), "head"),
            P("head", None),
            P(("groups", "seq", "inner"), None),
        ),
        out_specs=tokens,
        check_vma=False,
    )
```

```python
import functools

import jax
import jax.numpy as jnp
from jax import lax
from jax.experimental import pallas as pl
from jax.experimental.pallas import tpu as pltpu
from jax.sharding import PartitionSpec as P

BLK = 64
EXTRA = 16
F32 = jnp.float32
BF16 = jnp.bfloat16
NT = (((1,), (1,)), ((), ()))
TN = (((0,), (0,)), ((), ()))
NEG = -1e30
NEVER = 1 << 20
N_EARLY = 1
GROUPS = 4
VMEM = pl.BlockSpec(memory_space=pltpu.VMEM)
HBM = pl.BlockSpec(memory_space=pltpu.HBM)
SMEM = pl.BlockSpec(memory_space=pltpu.SMEM)
PARAMS = pltpu.CompilerParams(vmem_limit_bytes=48 * 2**20)


def iota(shape, dim):
    return lax.broadcasted_iota(jnp.int32, shape, dim)


def mm(a, b, dims=(((1,), (0,)), ((), ()))):
    return lax.dot_general(a, b, dims, preferred_element_type=F32)


def halves(x):
    hi = x.astype(BF16)
    return hi, (x - hi.astype(F32)).astype(BF16)


def pack_kernel(kv, keys, values, decay, out, kv_in, decay_in, even, sems):
    tokens = keys.shape[0] // kv
    copies = [
        pltpu.make_async_copy(keys, kv_in.at[0], sems.at[0]),
        pltpu.make_async_copy(values, kv_in.at[1], sems.at[1]),
        pltpu.make_async_copy(decay, decay_in, sems.at[2]),
    ]
    for c in copies:
        c.start()
    for n in range(2):
        copies[n].wait()
        even[...] = kv_in[n].astype(F32)
        for g in range(kv):
            at = (n * kv + g) * tokens
            out[at : at + tokens, :] = even[pl.ds(g, tokens, stride=kv), :].astype(BF16)
    copies[2].wait()
    left = jnp.maximum(decay_in[...], NEG)
    parts = []
    for _ in range(3):
        parts.append(left.astype(BF16).astype(F32))
        left = left - parts[-1]
    rest = jnp.zeros((EXTRA - 3 * kv, tokens), F32)
    out[2 * kv * tokens :, :] = jnp.concatenate([*parts, rest], axis=0).astype(BF16)


def parts_of(piece, kv):
    rows = piece[piece.shape[0] - EXTRA :, :].astype(F32)
    rest = jnp.zeros((8 - kv, rows.shape[1]), F32)
    return [jnp.concatenate([rows[n * kv : (n + 1) * kv], rest], axis=0) for n in range(3)]


def block_biases(number, per, blocks, b, tokens):
    block = number * per + iota((1, tokens), 1) // BLK
    listed = block == blocks[b, 0]
    for j in range(1, blocks.shape[1]):
        listed = jnp.logical_or(listed, block == blocks[b, j])
    return jnp.where(listed, 0.0, NEG)


def local_kernel(kv, numbers, queries, piece, blocks, gain, q_out, lin_out, grown_out, bias_out, gain_out, q_in, sems):
    copy = pltpu.make_async_copy(queries, q_in, sems.at[0])
    copy.start()
    gain_copy = pltpu.make_async_copy(gain, gain_out, sems.at[1])
    gain_copy.start()
    tokens, heads, width = queries.shape
    rep = heads // kv
    rows = tokens * rep
    per = blocks.shape[0]
    parts = [p.astype(BF16) for p in parts_of(piece, kv)]
    upto = iota((rows, tokens), 1) <= iota((rows, tokens), 0) // rep
    ones = jnp.where(upto, 1.0, 0.0).astype(BF16)
    ahead = jnp.where(iota((tokens, tokens), 0) <= iota((tokens, tokens), 1), 1.0, 0.0).astype(BF16)
    cum_row = mm(parts[0], ahead) + mm(parts[1], ahead) + mm(parts[2], ahead)
    cum_col = mm(ones, parts[0], NT) + mm(ones, parts[1], NT) + mm(ones, parts[2], NT)
    if numbers is not None:
        rows_of = [block_biases(n, per, blocks, b, tokens) for b in range(per) for n in numbers()]
        for r, row in enumerate(rows_of):
            bias_out[r : r + 1, :] = row
    copy.wait()
    qf = q_in[...].astype(F32)
    for g in range(kv):
        q = qf[:, g * rep : (g + 1) * rep, :].reshape(rows, width).astype(BF16)
        q_out[g] = q
        k = piece[g * tokens : (g + 1) * tokens, :]
        v = piece[(kv + g) * tokens : (kv + g + 1) * tokens, :]
        cum = jnp.broadcast_to(cum_col[:, g : g + 1], (rows, tokens))
        grown_out[g] = jnp.exp(cum)
        weight = jnp.where(upto, jnp.exp(jnp.minimum(cum - cum_row[g : g + 1, :], 0.0)), 0.0)
        hi, lo = halves(mm(q, k, NT) * weight)
        lin_out[g] = mm(hi, v) + mm(lo, v)
    gain_copy.wait()


def attend(kv, b, per, queries, pieces, biases, own, scores, out):
    _, rows, width = queries.shape
    part = rows // per
    factor = width**-0.5 * 1.4426950408889634
    tokens = scores.shape[1] // len(pieces)
    for g in range(kv):
        q = queries[g, b * part : (b + 1) * part, :]
        top = None
        for i, piece in enumerate(pieces):
            s = mm(q, piece[g * tokens : (g + 1) * tokens, :], NT) + biases[i]
            mask = own(i, (part, tokens))
            if mask is not None:
                s = jnp.where(mask, s, NEG)
            scores[:, i * tokens : (i + 1) * tokens] = s
            top = s if top is None else jnp.maximum(top, s)
        top = jnp.max(top, axis=1, keepdims=True)
        total, acc = None, None
        for i, piece in enumerate(pieces):
            e = jnp.exp2((scores[:, i * tokens : (i + 1) * tokens] - top) * factor)
            o = mm(e.astype(BF16), piece[(kv + g) * tokens : (kv + g + 1) * tokens, :])
            total = e if total is None else total + e
            acc = o if acc is None else acc + o
        out[g, b * part : (b + 1) * part, :] = acc / jnp.sum(total, axis=1, keepdims=True)


def suffixes(parts, tokens):
    after = jnp.where(iota((tokens, tokens), 1) > iota((tokens, tokens), 0), 1.0, 0.0).astype(BF16)
    hi, mid, lo = (p.astype(BF16) for p in parts)
    return mm(after, hi, NT) + mm(after, mid, NT) + mm(after, lo, NT)


def totals(parts):
    return jnp.sum(parts[0] + parts[1] + parts[2], axis=1, keepdims=True)


def own_states(kv, piece, suffix, shift):
    tokens = suffix.shape[0]
    result = []
    for g in range(kv):
        w = jnp.exp(jnp.minimum(suffix[:, g : g + 1] + shift[g], 0.0))
        k = piece[g * tokens : (g + 1) * tokens, :]
        hi, lo = halves(piece[(kv + g) * tokens : (kv + g + 1) * tokens, :].astype(F32) * w)
        both = mm(k, jnp.concatenate([hi, lo], axis=1), TN)
        width = hi.shape[1]
        result.append(both[:, :width] + both[:, width:])
    return result


def finish(kv, queries, lin, grown, sparse, gain, state, out, buffer, sems):
    tokens, heads, width = out.shape
    rep = heads // kv
    groups = sems.shape[0]
    each = tokens // groups
    split = [jnp.concatenate(halves(s), axis=1) for s in state]
    copies = []
    for n in range(groups):
        rows = slice(n * each * rep, (n + 1) * each * rep)
        here = slice(n * each, (n + 1) * each)
        both = []
        for g in range(kv):
            q = queries[g, rows, :]
            inter = mm(q, split[g])
            linear = lin[g, rows, :] + grown[g, rows, :] * (inter[:, :width] + inter[:, width:])
            mean = jnp.mean(linear * linear, axis=1, keepdims=True)
            normed = (linear * lax.rsqrt(mean + 1e-06)).reshape(each, rep, width)
            normed = normed * gain[g * rep : (g + 1) * rep, :][None]
            both.append(normed + sparse[g, rows, :].reshape(each, rep, width))
        buffer[here] = jnp.concatenate(both, axis=1).astype(BF16)
        copies.append(pltpu.make_async_copy(buffer.at[here], out.at[here], sems.at[n]))
        copies[-1].start()
    for c in copies:
        c.wait()


def column_kernel(kv, slots, ids, queries, blocks, column, out, scores):
    per = blocks.shape[0]
    tokens = per * BLK
    rep = queries.shape[1] // tokens
    here, number = ids()
    for b in range(per):

        def own(i, shape):
            position = here * tokens + b * BLK + iota(shape, 0) // rep
            return number(i) * tokens + iota(shape, 1) <= position

        biases = [block_biases(number(i), per, blocks, b, tokens) for i in range(slots)]
        attend(kv, b, per, queries, [column.at[i] for i in range(slots)], biases, own, scores, out)


def final_kernel(kv, slots, place, queries, lin, grown, sparse, gain, everything, out, buffer, sems):
    tokens = out.shape[0]
    width = queries.shape[2]

    def turn(n, carry):
        shift, state = carry
        at, keep = place(n)
        piece = everything.at[at]
        parts = parts_of(piece, kv)
        shifts = [shift[g : g + 1, :] for g in range(kv)]
        more = own_states(kv, piece, suffixes(parts, tokens), shifts)
        state = tuple(s + jnp.where(keep, m, 0.0) for s, m in zip(state, more))
        return shift + jnp.where(keep, totals(parts), 0.0), state

    zero = tuple(jnp.zeros((width, width), F32) for _ in range(kv))
    _, state = lax.fori_loop(0, slots, turn, (jnp.zeros((8, 1), F32), zero))
    finish(kv, queries, lin, grown, sparse, gain, state, out, buffer, sems)


def add_between(shift, i, far, sums):
    for j, total in sums:
        if j != i:
            shift = shift + jnp.where(far[j] < far[i], total, 0.0)
    return shift


def sparse_kernel(kv, n_column, per, distance, queries, biases, *refs):
    *pieces, out, states, shifts, scores = refs
    column = pieces[:n_column]
    tokens = per * BLK
    rep = queries.shape[1] // tokens
    far = distance()
    parts = [parts_of(p, kv) for p in pieces[1:]]
    suffix = suffixes([jnp.concatenate(p, axis=0) for p in zip(*parts)], tokens)
    sums = [(i, totals(p)) for i, p in enumerate(parts)]
    for i in range(len(far)):
        shift = add_between(jnp.zeros((8, 1), F32), i, far, sums)
        shifts[8 * i : 8 * i + 8, :] = jnp.broadcast_to(shift, (8, shifts.shape[1]))
    for i, piece in enumerate(pieces[1:]):
        for g, state in enumerate(own_states(kv, piece, suffix[:, 8 * i : 8 * i + 8], [0.0] * kv)):
            states[i * kv + g] = state
    for b in range(per):

        def own(i, shape):
            return iota(shape, 1) <= b * BLK + iota(shape, 0) // rep if i == 0 else None

        rows = [biases[b * n_column + i : b * n_column + i + 1, :] for i in range(n_column)]
        attend(kv, b, per, queries, column, rows, own, scores, out)


def last_kernel(kv, distance, queries, lin, grown, sparse, gain, states, shifts, *refs):
    *late, out, buffer, sems = refs
    far = distance()
    early = len(far) - len(late)
    tokens = out.shape[0]
    parts = [parts_of(p, kv) for p in late]
    suffix = suffixes([jnp.concatenate(p, axis=0) for p in zip(*parts)], tokens)
    sums = [(early + n, totals(p)) for n, p in enumerate(parts)]
    mine = [own_states(kv, p, suffix[:, 8 * n : 8 * n + 8], [0.0] * kv) for n, p in enumerate(late)]
    state = [0.0] * kv
    for i in range(len(far)):
        shift = add_between(shifts[8 * i : 8 * i + 8, :], i, far, sums)
        factor = jnp.where(far[i] < NEVER, jnp.exp(jnp.minimum(shift, 0.0)), 0.0)
        for g in range(kv):
            piece_state = states[i * kv + g] if i < early else mine[i - early][g]
            state[g] = state[g] + factor[g : g + 1, :] * piece_state
    finish(kv, queries, lin, grown, sparse, gain, state, out, buffer, sems)


def where_am_i():
    return lax.axis_index("seq"), lax.axis_index("inner")


def pick(table, at):
    value = jnp.int32(table[0])
    for n in range(1, len(table)):
        value = jnp.where(at == n, table[n], value)
    return value


def in_hbm(x):
    return pltpu.with_memory_space_constraint(x, pltpu.HBM)


def shards(queries, keys, values, log_decay, gain, block_list):
    tokens, heads, width = queries.shape
    kv = keys.shape[1]
    rows = tokens * (heads // kv)
    per = tokens // BLK
    n_seq, n_inner = lax.axis_size("seq"), lax.axis_size("inner")
    shape = jax.ShapeDtypeStruct

    def call(kernel, out_shape, in_specs, scratch, *args, cost=None, out_specs=None):
        one = not isinstance(out_shape, tuple)
        return pl.pallas_call(
            kernel,
            out_shape=out_shape,
            in_specs=in_specs,
            out_specs=out_specs or (VMEM if one else tuple(VMEM for _ in out_shape)),
            scratch_shapes=scratch,
            compiler_params=PARAMS,
            cost_estimate=cost,
        )(*args)

    piece = call(
        functools.partial(pack_kernel, kv),
        shape((2 * kv * tokens + EXTRA, width), BF16),
        [HBM] * 3,
        [
            pltpu.VMEM((2, kv * tokens, width), BF16),
            pltpu.VMEM((kv, tokens), F32),
            pltpu.VMEM((kv * tokens, width), F32),
            pltpu.SemaphoreType.DMA((3,)),
        ],
        in_hbm(keys.reshape(-1, width)),
        in_hbm(values.reshape(-1, width)),
        in_hbm(log_decay.T),
    )
    few = n_seq == 4 and n_inner == 2

    def numbers():
        z, x = where_am_i()
        found = [z * n_inner + x]
        for table in held:
            other = pick(table, z)
            found.append(jnp.where(other < z, other * n_inner + x, -1))
        return found

    def distance():
        z, x = where_am_i()
        mine, theirs = [], [jnp.where(x == 1, 1, NEVER)]
        for table in held:
            other = pick(table, z)
            mine.append(jnp.where(other < z, (z - other) * n_inner, NEVER))
            theirs.append(jnp.where(other < z, (z - other) * n_inner + jnp.where(x == 1, 1, -1), NEVER))
        return mine + theirs

    if few:
        first, second, third = (
            [(0, 2), (2, 3), (1, 1), (3, 0)],
            [(0, 1), (1, 3), (3, 2), (2, 0)],
            [(1, 2), (2, 3)],
        )
        came = [{b: a for a, b in pairs} for pairs in (first, second, third)]
        held = [
            [came[0].get(i, n_seq) for i in range(4)],
            [came[1].get(i, n_seq) for i in range(4)],
            [came[0].get(came[2].get(i, n_seq), n_seq) for i in range(4)],
        ]

    q, lin, grown, biases, gain = call(
        functools.partial(local_kernel, kv, numbers if few else None),
        (
            shape((kv, rows, width), BF16),
            shape((kv, rows, width), F32),
            shape((kv, rows, tokens), F32),
            shape((8, tokens), F32),
            shape(gain.shape, F32),
        ),
        [HBM, VMEM, SMEM, HBM],
        [pltpu.VMEM(queries.shape, BF16), pltpu.SemaphoreType.DMA((2,))],
        in_hbm(queries),
        piece,
        block_list,
        in_hbm(gain),
        cost=pl.CostEstimate(flops=4 * 10**9, bytes_accessed=4 * 10**6, transcendentals=10**6),
    )
    if few:

        def swap(x):
            return lax.ppermute(x, "inner", [(0, 1), (1, 0)])

        theirs = swap(piece)
        got1 = lax.ppermute(piece, "seq", first)
        got2 = lax.ppermute(piece, "seq", second)
        got1, q, theirs = lax.optimization_barrier((got1, q, theirs))
        theirs1 = swap(got1)
        got3 = lax.ppermute(got1, "seq", third)
        column = [piece, got1, got2, got3]
        other = [theirs, theirs1, swap(got2), swap(got3)]

    out_shape = shape((tokens, heads, width), BF16)
    write_out = [pltpu.VMEM(out_shape.shape, BF16), pltpu.SemaphoreType.DMA((GROUPS,))]
    if few:
        early = column[1:] + other[:N_EARLY]
        late = other[N_EARLY:]
        sparse, states, shifts = call(
            functools.partial(sparse_kernel, kv, n_seq, per, distance),
            (
                shape((kv, rows, width), F32),
                shape((len(early) * kv, width, width), F32),
                shape(((len(early) + len(late)) * 8, width), F32),
            ),
            [VMEM] * (3 + len(early)),
            [pltpu.VMEM((rows // per, n_seq * tokens), F32)],
            q,
            biases,
            piece,
            *early,
        )
        return call(
            functools.partial(last_kernel, kv, distance),
            out_shape,
            [VMEM] * (7 + len(late)),
            write_out,
            q,
            lin,
            grown,
            sparse,
            gain,
            states,
            shifts,
            *late,
            out_specs=HBM,
        )

    column = lax.all_gather(piece, "seq")
    everything = lax.all_gather(column, "inner").reshape(n_inner * n_seq, *piece.shape)

    def ids():
        z, x = where_am_i()
        return z * n_inner + x, lambda i: i * n_inner + x

    def place(n):
        z, x = where_am_i()
        p = n_seq * n_inner - 1 - n
        return lax.rem(p, n_inner) * n_seq + lax.div(p, n_inner), p < z * n_inner + x

    sparse = call(
        functools.partial(column_kernel, kv, n_seq, ids),
        shape((kv, rows, width), F32),
        [VMEM, SMEM, VMEM],
        [pltpu.VMEM((rows // per, n_seq * tokens), F32)],
        q,
        block_list,
        column,
    )
    return call(
        functools.partial(final_kernel, kv, n_seq * n_inner, place),
        out_shape,
        [VMEM] * 6,
        write_out,
        q,
        lin,
        grown,
        sparse,
        gain,
        everything,
        out_specs=HBM,
    )


def solution(mesh):
    tokens = P(("groups", "seq", "inner"), "head", None)
    return jax.shard_map(
        shards,
        mesh=mesh,
        in_specs=(
            tokens,
            tokens,
            tokens,
            P(("groups", "seq", "inner"), "head"),
            P("head", None),
            P(("groups", "seq", "inner"), None),
        ),
        out_specs=tokens,
        check_vma=False,
    )
```

```python
import functools

import jax
import jax.numpy as jnp
from jax import lax
from jax.experimental import pallas as pl
from jax.experimental.pallas import tpu as pltpu
from jax.sharding import PartitionSpec as P

BLK = 64
EXTRA = 16
F32 = jnp.float32
BF16 = jnp.bfloat16
NT = (((1,), (1,)), ((), ()))
TN = (((0,), (0,)), ((), ()))
NEG = -1e30
NEVER = 1 << 20
N_EARLY = 1
GROUPS = 4
VMEM = pl.BlockSpec(memory_space=pltpu.VMEM)
HBM = pl.BlockSpec(memory_space=pltpu.HBM)
SMEM = pl.BlockSpec(memory_space=pltpu.SMEM)
PARAMS = pltpu.CompilerParams(vmem_limit_bytes=48 * 2**20)


def iota(shape, dim):
    return lax.broadcasted_iota(jnp.int32, shape, dim)


def mm(a, b, dims=(((1,), (0,)), ((), ()))):
    return lax.dot_general(a, b, dims, preferred_element_type=F32)


def halves(x):
    hi = x.astype(BF16)
    return hi, (x - hi.astype(F32)).astype(BF16)


def pack_kernel(kv, keys, values, decay, out, kv_in, decay_in, even, sems):
    tokens = keys.shape[0] // kv
    copies = [
        pltpu.make_async_copy(keys, kv_in.at[0], sems.at[0]),
        pltpu.make_async_copy(values, kv_in.at[1], sems.at[1]),
        pltpu.make_async_copy(decay, decay_in, sems.at[2]),
    ]
    for c in copies:
        c.start()
    for n in range(2):
        copies[n].wait()
        even[...] = kv_in[n].astype(F32)
        for g in range(kv):
            at = (n * kv + g) * tokens
            out[at : at + tokens, :] = even[pl.ds(g, tokens, stride=kv), :].astype(BF16)
    copies[2].wait()
    left = jnp.maximum(decay_in[...], NEG)
    parts = []
    for _ in range(3):
        parts.append(left.astype(BF16).astype(F32))
        left = left - parts[-1]
    rest = jnp.zeros((EXTRA - 3 * kv, tokens), F32)
    out[2 * kv * tokens :, :] = jnp.concatenate([*parts, rest], axis=0).astype(BF16)


def parts_of(piece, kv):
    rows = piece[piece.shape[0] - EXTRA :, :].astype(F32)
    rest = jnp.zeros((8 - kv, rows.shape[1]), F32)
    return [jnp.concatenate([rows[n * kv : (n + 1) * kv], rest], axis=0) for n in range(3)]


def block_biases(number, per, blocks, b, tokens):
    block = number * per + iota((1, tokens), 1) // BLK
    listed = block == blocks[b, 0]
    for j in range(1, blocks.shape[1]):
        listed = jnp.logical_or(listed, block == blocks[b, j])
    return jnp.where(listed, 0.0, NEG)


def local_kernel(kv, numbers, queries, piece, blocks, gain, q_out, lin_out, grown_out, bias_out, gain_out, q_in, sems):
    copy = pltpu.make_async_copy(queries, q_in, sems.at[0])
    copy.start()
    gain_copy = pltpu.make_async_copy(gain, gain_out, sems.at[1])
    gain_copy.start()
    tokens, heads, width = queries.shape
    rep = heads // kv
    rows = tokens * rep
    per = blocks.shape[0]
    parts = [p.astype(BF16) for p in parts_of(piece, kv)]
    upto = iota((rows, tokens), 1) <= iota((rows, tokens), 0) // rep
    ones = jnp.where(upto, 1.0, 0.0).astype(BF16)
    ahead = jnp.where(iota((tokens, tokens), 0) <= iota((tokens, tokens), 1), 1.0, 0.0).astype(BF16)
    cum_row = mm(parts[0], ahead) + mm(parts[1], ahead) + mm(parts[2], ahead)
    cum_col = mm(ones, parts[0], NT) + mm(ones, parts[1], NT) + mm(ones, parts[2], NT)
    if numbers is not None:
        rows_of = [block_biases(n, per, blocks, b, tokens) for b in range(per) for n in numbers()]
        for r, row in enumerate(rows_of):
            bias_out[r : r + 1, :] = row
    copy.wait()
    qf = q_in[...].astype(F32)
    for g in range(kv):
        q = qf[:, g * rep : (g + 1) * rep, :].reshape(rows, width).astype(BF16)
        q_out[g] = q
        k = piece[g * tokens : (g + 1) * tokens, :]
        v = piece[(kv + g) * tokens : (kv + g + 1) * tokens, :]
        cum = jnp.broadcast_to(cum_col[:, g : g + 1], (rows, tokens))
        grown_out[g] = jnp.exp(cum)
        weight = jnp.where(upto, jnp.exp(jnp.minimum(cum - cum_row[g : g + 1, :], 0.0)), 0.0)
        both = jnp.concatenate(halves(mm(q, k, NT) * weight), axis=1)
        lin_out[g] = mm(both, jnp.concatenate([v, v], axis=0))
    gain_copy.wait()


def attend(kv, b, per, queries, pieces, biases, own, scores, out):
    _, rows, width = queries.shape
    part = rows // per
    factor = width**-0.5 * 1.4426950408889634
    tokens = scores.shape[1] // len(pieces)
    for g in range(kv):
        q = queries[g, b * part : (b + 1) * part, :]
        top = None
        for i, piece in enumerate(pieces):
            s = mm(q, piece[g * tokens : (g + 1) * tokens, :], NT) + biases[i]
            mask = own(i, (part, tokens))
            if mask is not None:
                s = jnp.where(mask, s, NEG)
            scores[:, i * tokens : (i + 1) * tokens] = s
            top = s if top is None else jnp.maximum(top, s)
        top = jnp.max(top, axis=1, keepdims=True)
        total, acc = None, None
        for i, piece in enumerate(pieces):
            e = jnp.exp2((scores[:, i * tokens : (i + 1) * tokens] - top) * factor)
            o = mm(e.astype(BF16), piece[(kv + g) * tokens : (kv + g + 1) * tokens, :])
            total = e if total is None else total + e
            acc = o if acc is None else acc + o
        out[g, b * part : (b + 1) * part, :] = acc / jnp.sum(total, axis=1, keepdims=True)


def suffixes(parts, tokens):
    after = jnp.where(iota((tokens, tokens), 1) > iota((tokens, tokens), 0), 1.0, 0.0).astype(BF16)
    hi, mid, lo = (p.astype(BF16) for p in parts)
    return mm(after, hi, NT) + mm(after, mid, NT) + mm(after, lo, NT)


def totals(parts):
    return jnp.sum(parts[0] + parts[1] + parts[2], axis=1, keepdims=True)


def own_states(kv, piece, suffix, shift):
    tokens = suffix.shape[0]
    result = []
    for g in range(kv):
        w = jnp.exp(jnp.minimum(suffix[:, g : g + 1] + shift[g], 0.0))
        k = piece[g * tokens : (g + 1) * tokens, :]
        hi, lo = halves(piece[(kv + g) * tokens : (kv + g + 1) * tokens, :].astype(F32) * w)
        both = mm(k, jnp.concatenate([hi, lo], axis=1), TN)
        width = hi.shape[1]
        result.append(both[:, :width] + both[:, width:])
    return result


def finish(kv, queries, lin, grown, sparse, gain, state, out, buffer, sems):
    tokens, heads, width = out.shape
    rep = heads // kv
    groups = sems.shape[0]
    each = tokens // groups
    split = [jnp.concatenate(halves(s), axis=0) for s in state]
    copies = []
    for n in range(groups):
        rows = slice(n * each * rep, (n + 1) * each * rep)
        here = slice(n * each, (n + 1) * each)
        both = []
        for g in range(kv):
            q = queries[g, rows, :]
            inter = mm(jnp.concatenate([q, q], axis=1), split[g])
            linear = lin[g, rows, :] + grown[g, rows, :] * inter
            mean = jnp.mean(linear * linear, axis=1, keepdims=True)
            normed = (linear * lax.rsqrt(mean + 1e-06)).reshape(each, rep, width)
            normed = normed * gain[g * rep : (g + 1) * rep, :][None]
            both.append(normed + sparse[g, rows, :].reshape(each, rep, width))
        buffer[here] = jnp.concatenate(both, axis=1).astype(BF16)
        copies.append(pltpu.make_async_copy(buffer.at[here], out.at[here], sems.at[n]))
        copies[-1].start()
    for c in copies:
        c.wait()


def column_kernel(kv, slots, ids, queries, blocks, column, out, scores):
    per = blocks.shape[0]
    tokens = per * BLK
    rep = queries.shape[1] // tokens
    here, number = ids()
    for b in range(per):

        def own(i, shape):
            position = here * tokens + b * BLK + iota(shape, 0) // rep
            return number(i) * tokens + iota(shape, 1) <= position

        biases = [block_biases(number(i), per, blocks, b, tokens) for i in range(slots)]
        attend(kv, b, per, queries, [column.at[i] for i in range(slots)], biases, own, scores, out)


def final_kernel(kv, slots, place, queries, lin, grown, sparse, gain, everything, out, buffer, sems):
    tokens = out.shape[0]
    width = queries.shape[2]

    def turn(n, carry):
        shift, state = carry
        at, keep = place(n)
        piece = everything.at[at]
        parts = parts_of(piece, kv)
        shifts = [shift[g : g + 1, :] for g in range(kv)]
        more = own_states(kv, piece, suffixes(parts, tokens), shifts)
        state = tuple(s + jnp.where(keep, m, 0.0) for s, m in zip(state, more))
        return shift + jnp.where(keep, totals(parts), 0.0), state

    zero = tuple(jnp.zeros((width, width), F32) for _ in range(kv))
    _, state = lax.fori_loop(0, slots, turn, (jnp.zeros((8, 1), F32), zero))
    finish(kv, queries, lin, grown, sparse, gain, state, out, buffer, sems)


def add_between(shift, i, far, sums):
    for j, total in sums:
        if j != i:
            shift = shift + jnp.where(far[j] < far[i], total, 0.0)
    return shift


def sparse_kernel(kv, n_column, per, distance, queries, biases, *refs):
    *pieces, out, states, shifts, scores = refs
    column = pieces[:n_column]
    tokens = per * BLK
    rep = queries.shape[1] // tokens
    far = distance()
    parts = [parts_of(p, kv) for p in pieces[1:]]
    suffix = suffixes([jnp.concatenate(p, axis=0) for p in zip(*parts)], tokens)
    sums = [(i, totals(p)) for i, p in enumerate(parts)]
    for i in range(len(far)):
        shift = add_between(jnp.zeros((8, 1), F32), i, far, sums)
        shifts[8 * i : 8 * i + 8, :] = jnp.broadcast_to(shift, (8, shifts.shape[1]))
    for i, piece in enumerate(pieces[1:]):
        for g, state in enumerate(own_states(kv, piece, suffix[:, 8 * i : 8 * i + 8], [0.0] * kv)):
            states[i * kv + g] = state
    for b in range(per):

        def own(i, shape):
            return iota(shape, 1) <= b * BLK + iota(shape, 0) // rep if i == 0 else None

        rows = [biases[b * n_column + i : b * n_column + i + 1, :] for i in range(n_column)]
        attend(kv, b, per, queries, column, rows, own, scores, out)


def last_kernel(kv, distance, queries, lin, grown, sparse, gain, states, shifts, *refs):
    *late, out, buffer, sems = refs
    far = distance()
    early = len(far) - len(late)
    tokens = out.shape[0]
    parts = [parts_of(p, kv) for p in late]
    suffix = suffixes([jnp.concatenate(p, axis=0) for p in zip(*parts)], tokens)
    sums = [(early + n, totals(p)) for n, p in enumerate(parts)]
    mine = [own_states(kv, p, suffix[:, 8 * n : 8 * n + 8], [0.0] * kv) for n, p in enumerate(late)]
    state = [0.0] * kv
    for i in range(len(far)):
        shift = add_between(shifts[8 * i : 8 * i + 8, :], i, far, sums)
        factor = jnp.where(far[i] < NEVER, jnp.exp(jnp.minimum(shift, 0.0)), 0.0)
        for g in range(kv):
            piece_state = states[i * kv + g] if i < early else mine[i - early][g]
            state[g] = state[g] + factor[g : g + 1, :] * piece_state
    finish(kv, queries, lin, grown, sparse, gain, state, out, buffer, sems)


def where_am_i():
    return lax.axis_index("seq"), lax.axis_index("inner")


def pick(table, at):
    value = jnp.int32(table[0])
    for n in range(1, len(table)):
        value = jnp.where(at == n, table[n], value)
    return value


def in_hbm(x):
    return pltpu.with_memory_space_constraint(x, pltpu.HBM)


def shards(queries, keys, values, log_decay, gain, block_list):
    tokens, heads, width = queries.shape
    kv = keys.shape[1]
    rows = tokens * (heads // kv)
    per = tokens // BLK
    n_seq, n_inner = lax.axis_size("seq"), lax.axis_size("inner")
    shape = jax.ShapeDtypeStruct

    def call(kernel, out_shape, in_specs, scratch, *args, cost=None, out_specs=None):
        one = not isinstance(out_shape, tuple)
        return pl.pallas_call(
            kernel,
            out_shape=out_shape,
            in_specs=in_specs,
            out_specs=out_specs or (VMEM if one else tuple(VMEM for _ in out_shape)),
            scratch_shapes=scratch,
            compiler_params=PARAMS,
            cost_estimate=cost,
        )(*args)

    piece = call(
        functools.partial(pack_kernel, kv),
        shape((2 * kv * tokens + EXTRA, width), BF16),
        [HBM] * 3,
        [
            pltpu.VMEM((2, kv * tokens, width), BF16),
            pltpu.VMEM((kv, tokens), F32),
            pltpu.VMEM((kv * tokens, width), F32),
            pltpu.SemaphoreType.DMA((3,)),
        ],
        in_hbm(keys.reshape(-1, width)),
        in_hbm(values.reshape(-1, width)),
        in_hbm(log_decay.T),
    )
    few = n_seq == 4 and n_inner == 2

    def numbers():
        z, x = where_am_i()
        found = [z * n_inner + x]
        for table in held:
            other = pick(table, z)
            found.append(jnp.where(other < z, other * n_inner + x, -1))
        return found

    def distance():
        z, x = where_am_i()
        mine, theirs = [], [jnp.where(x == 1, 1, NEVER)]
        for table in held:
            other = pick(table, z)
            mine.append(jnp.where(other < z, (z - other) * n_inner, NEVER))
            theirs.append(jnp.where(other < z, (z - other) * n_inner + jnp.where(x == 1, 1, -1), NEVER))
        return mine + theirs

    if few:
        first, second, third = (
            [(0, 2), (2, 3), (1, 1)],
            [(0, 1), (1, 3), (3, 2), (2, 0)],
            [(1, 2), (2, 3)],
        )
        came = [{b: a for a, b in pairs} for pairs in (first, second, third)]
        held = [
            [came[0].get(i, n_seq) for i in range(4)],
            [came[1].get(i, n_seq) for i in range(4)],
            [came[0].get(came[2].get(i, n_seq), n_seq) for i in range(4)],
        ]

    q, lin, grown, biases, gain = call(
        functools.partial(local_kernel, kv, numbers if few else None),
        (
            shape((kv, rows, width), BF16),
            shape((kv, rows, width), F32),
            shape((kv, rows, tokens), F32),
            shape((8, tokens), F32),
            shape(gain.shape, F32),
        ),
        [HBM, VMEM, SMEM, HBM],
        [pltpu.VMEM(queries.shape, BF16), pltpu.SemaphoreType.DMA((2,))],
        in_hbm(queries),
        piece,
        block_list,
        in_hbm(gain),
        cost=pl.CostEstimate(flops=4 * 10**9, bytes_accessed=4 * 10**6, transcendentals=10**6),
    )
    if few:

        def swap(x):
            return lax.ppermute(x, "inner", [(0, 1), (1, 0)])

        theirs = swap(piece)
        got1 = lax.ppermute(piece, "seq", first)
        got2 = lax.ppermute(piece, "seq", second)
        got1, q, theirs = lax.optimization_barrier((got1, q, theirs))
        theirs1 = swap(got1)
        got3 = lax.ppermute(got1, "seq", third)
        column = [piece, got1, got2, got3]
        other = [theirs, theirs1, swap(got2), swap(got3)]

    out_shape = shape((tokens, heads, width), BF16)
    write_out = [pltpu.VMEM(out_shape.shape, BF16), pltpu.SemaphoreType.DMA((GROUPS,))]
    if few:
        early = column[1:] + other[:N_EARLY]
        late = other[N_EARLY:]
        sparse, states, shifts = call(
            functools.partial(sparse_kernel, kv, n_seq, per, distance),
            (
                shape((kv, rows, width), F32),
                shape((len(early) * kv, width, width), F32),
                shape(((len(early) + len(late)) * 8, width), F32),
            ),
            [VMEM] * (3 + len(early)),
            [pltpu.VMEM((rows // per, n_seq * tokens), F32)],
            q,
            biases,
            piece,
            *early,
        )
        return call(
            functools.partial(last_kernel, kv, distance),
            out_shape,
            [VMEM] * (7 + len(late)),
            write_out,
            q,
            lin,
            grown,
            sparse,
            gain,
            states,
            shifts,
            *late,
            out_specs=HBM,
        )

    column = lax.all_gather(piece, "seq")
    everything = lax.all_gather(column, "inner").reshape(n_inner * n_seq, *piece.shape)

    def ids():
        z, x = where_am_i()
        return z * n_inner + x, lambda i: i * n_inner + x

    def place(n):
        z, x = where_am_i()
        p = n_seq * n_inner - 1 - n
        return lax.rem(p, n_inner) * n_seq + lax.div(p, n_inner), p < z * n_inner + x

    sparse = call(
        functools.partial(column_kernel, kv, n_seq, ids),
        shape((kv, rows, width), F32),
        [VMEM, SMEM, VMEM],
        [pltpu.VMEM((rows // per, n_seq * tokens), F32)],
        q,
        block_list,
        column,
    )
    return call(
        functools.partial(final_kernel, kv, n_seq * n_inner, place),
        out_shape,
        [VMEM] * 6,
        write_out,
        q,
        lin,
        grown,
        sparse,
        gain,
        everything,
        out_specs=HBM,
    )


def solution(mesh):
    tokens = P(("groups", "seq", "inner"), "head", None)
    return jax.shard_map(
        shards,
        mesh=mesh,
        in_specs=(
            tokens,
            tokens,
            tokens,
            P(("groups", "seq", "inner"), "head"),
            P("head", None),
            P(("groups", "seq", "inner"), None),
        ),
        out_specs=tokens,
        check_vma=False,
    )
```

```python
import functools

import jax
import jax.numpy as jnp
from jax import lax
from jax.experimental import pallas as pl
from jax.experimental.pallas import tpu as pltpu
from jax.sharding import PartitionSpec as P

BLK = 64
EXTRA = 16
F32 = jnp.float32
BF16 = jnp.bfloat16
NT = (((1,), (1,)), ((), ()))
TN = (((0,), (0,)), ((), ()))
NEG = -1e30
NEVER = 1 << 20
N_EARLY = 1
GROUPS = 4
VMEM = pl.BlockSpec(memory_space=pltpu.VMEM)
HBM = pl.BlockSpec(memory_space=pltpu.HBM)
SMEM = pl.BlockSpec(memory_space=pltpu.SMEM)
PARAMS = pltpu.CompilerParams(vmem_limit_bytes=48 * 2**20)


def iota(shape, dim):
    return lax.broadcasted_iota(jnp.int32, shape, dim)


def mm(a, b, dims=(((1,), (0,)), ((), ()))):
    return lax.dot_general(a, b, dims, preferred_element_type=F32)


def halves(x):
    hi = x.astype(BF16)
    return hi, (x - hi.astype(F32)).astype(BF16)


def pack_kernel(kv, keys, values, decay, out, kv_in, decay_in, even, sems):
    tokens = keys.shape[0] // kv
    copies = [
        pltpu.make_async_copy(keys, kv_in.at[0], sems.at[0]),
        pltpu.make_async_copy(values, kv_in.at[1], sems.at[1]),
        pltpu.make_async_copy(decay, decay_in, sems.at[2]),
    ]
    for c in copies:
        c.start()
    for n in range(2):
        copies[n].wait()
        even[...] = kv_in[n].astype(F32)
        for g in range(kv):
            at = (n * kv + g) * tokens
            out[at : at + tokens, :] = even[pl.ds(g, tokens, stride=kv), :].astype(BF16)
    copies[2].wait()
    left = jnp.maximum(decay_in[...], NEG)
    parts = []
    for _ in range(3):
        parts.append(left.astype(BF16).astype(F32))
        left = left - parts[-1]
    rest = jnp.zeros((EXTRA - 3 * kv, tokens), F32)
    out[2 * kv * tokens :, :] = jnp.concatenate([*parts, rest], axis=0).astype(BF16)


def parts_of(piece, kv):
    rows = piece[piece.shape[0] - EXTRA :, :].astype(F32)
    rest = jnp.zeros((8 - kv, rows.shape[1]), F32)
    return [jnp.concatenate([rows[n * kv : (n + 1) * kv], rest], axis=0) for n in range(3)]


def block_biases(number, per, blocks, b, tokens):
    block = number * per + iota((1, tokens), 1) // BLK
    listed = block == blocks[b, 0]
    for j in range(1, blocks.shape[1]):
        listed = jnp.logical_or(listed, block == blocks[b, j])
    return jnp.where(listed, 0.0, NEG)


def local_kernel(kv, numbers, queries, piece, blocks, gain, q_out, lin_out, grown_out, bias_out, gain_out, q_in, sems):
    copy = pltpu.make_async_copy(queries, q_in, sems.at[0])
    copy.start()
    gain_copy = pltpu.make_async_copy(gain, gain_out, sems.at[1])
    gain_copy.start()
    tokens, heads, width = queries.shape
    rep = heads // kv
    rows = tokens * rep
    per = blocks.shape[0]
    parts = [p.astype(BF16) for p in parts_of(piece, kv)]
    upto = iota((rows, tokens), 1) <= iota((rows, tokens), 0) // rep
    ones = jnp.where(upto, 1.0, 0.0).astype(BF16)
    ahead = jnp.where(iota((tokens, tokens), 0) <= iota((tokens, tokens), 1), 1.0, 0.0).astype(BF16)
    cum_row = mm(parts[0], ahead) + mm(parts[1], ahead) + mm(parts[2], ahead)
    cum_col = mm(ones, parts[0], NT) + mm(ones, parts[1], NT) + mm(ones, parts[2], NT)
    if numbers is not None:
        rows_of = [block_biases(n, per, blocks, b, tokens) for b in range(per) for n in numbers()]
        for r, row in enumerate(rows_of):
            bias_out[r : r + 1, :] = row
    copy.wait()
    qf = q_in[...].astype(F32)
    for g in range(kv):
        q = qf[:, g * rep : (g + 1) * rep, :].reshape(rows, width).astype(BF16)
        q_out[g] = q
        k = piece[g * tokens : (g + 1) * tokens, :]
        v = piece[(kv + g) * tokens : (kv + g + 1) * tokens, :]
        cum = jnp.broadcast_to(cum_col[:, g : g + 1], (rows, tokens))
        grown_out[g] = jnp.exp(cum)
        weight = jnp.where(upto, jnp.exp(jnp.minimum(cum - cum_row[g : g + 1, :], 0.0)), 0.0)
        both = jnp.concatenate(halves(mm(q, k, NT) * weight), axis=1)
        lin_out[g] = mm(both, jnp.concatenate([v, v], axis=0))
    gain_copy.wait()


def attend(kv, b, per, queries, pieces, biases, own, scores, out):
    _, rows, width = queries.shape
    part = rows // per
    factor = width**-0.5 * 1.4426950408889634
    tokens = scores.shape[1] // len(pieces)
    for g in range(kv):
        q = queries[g, b * part : (b + 1) * part, :]
        top = None
        for i, piece in enumerate(pieces):
            s = mm(q, piece[g * tokens : (g + 1) * tokens, :], NT) + biases[i]
            mask = own(i, (part, tokens))
            if mask is not None:
                s = jnp.where(mask, s, NEG)
            scores[:, i * tokens : (i + 1) * tokens] = s
            top = s if top is None else jnp.maximum(top, s)
        top = jnp.max(top, axis=1, keepdims=True)
        total, weights, vals = None, [], []
        for i, piece in enumerate(pieces):
            e = jnp.exp2((scores[:, i * tokens : (i + 1) * tokens] - top) * factor)
            weights.append(e.astype(BF16))
            vals.append(piece[(kv + g) * tokens : (kv + g + 1) * tokens, :])
            total = e if total is None else total + e
        acc = mm(jnp.concatenate(weights, axis=1), jnp.concatenate(vals, axis=0))
        out[g, b * part : (b + 1) * part, :] = acc / jnp.sum(total, axis=1, keepdims=True)


def suffixes(parts, tokens):
    after = jnp.where(iota((tokens, tokens), 1) > iota((tokens, tokens), 0), 1.0, 0.0).astype(BF16)
    hi, mid, lo = (p.astype(BF16) for p in parts)
    return mm(after, hi, NT) + mm(after, mid, NT) + mm(after, lo, NT)


def totals(parts):
    return jnp.sum(parts[0] + parts[1] + parts[2], axis=1, keepdims=True)


def own_states(kv, piece, suffix, shift):
    tokens = suffix.shape[0]
    result = []
    for g in range(kv):
        w = jnp.exp(jnp.minimum(suffix[:, g : g + 1] + shift[g], 0.0))
        k = piece[g * tokens : (g + 1) * tokens, :]
        hi, lo = halves(piece[(kv + g) * tokens : (kv + g + 1) * tokens, :].astype(F32) * w)
        both = mm(k, jnp.concatenate([hi, lo], axis=1), TN)
        width = hi.shape[1]
        result.append(both[:, :width] + both[:, width:])
    return result


def finish(kv, queries, lin, grown, sparse, gain, state, out, buffer, sems):
    tokens, heads, width = out.shape
    rep = heads // kv
    groups = sems.shape[0]
    each = tokens // groups
    split = [jnp.concatenate(halves(s), axis=0) for s in state]
    copies = []
    for n in range(groups):
        rows = slice(n * each * rep, (n + 1) * each * rep)
        here = slice(n * each, (n + 1) * each)
        both = []
        for g in range(kv):
            q = queries[g, rows, :]
            inter = mm(jnp.concatenate([q, q], axis=1), split[g])
            linear = lin[g, rows, :] + grown[g, rows, :] * inter
            mean = jnp.mean(linear * linear, axis=1, keepdims=True)
            normed = (linear * lax.rsqrt(mean + 1e-06)).reshape(each, rep, width)
            normed = normed * gain[g * rep : (g + 1) * rep, :][None]
            both.append(normed + sparse[g, rows, :].reshape(each, rep, width))
        buffer[here] = jnp.concatenate(both, axis=1).astype(BF16)
        copies.append(pltpu.make_async_copy(buffer.at[here], out.at[here], sems.at[n]))
        copies[-1].start()
    for c in copies:
        c.wait()


def column_kernel(kv, slots, ids, queries, blocks, column, out, scores):
    per = blocks.shape[0]
    tokens = per * BLK
    rep = queries.shape[1] // tokens
    here, number = ids()
    for b in range(per):

        def own(i, shape):
            position = here * tokens + b * BLK + iota(shape, 0) // rep
            return number(i) * tokens + iota(shape, 1) <= position

        biases = [block_biases(number(i), per, blocks, b, tokens) for i in range(slots)]
        attend(kv, b, per, queries, [column.at[i] for i in range(slots)], biases, own, scores, out)


def final_kernel(kv, slots, place, queries, lin, grown, sparse, gain, everything, out, buffer, sems):
    tokens = out.shape[0]
    width = queries.shape[2]

    def turn(n, carry):
        shift, state = carry
        at, keep = place(n)
        piece = everything.at[at]
        parts = parts_of(piece, kv)
        shifts = [shift[g : g + 1, :] for g in range(kv)]
        more = own_states(kv, piece, suffixes(parts, tokens), shifts)
        state = tuple(s + jnp.where(keep, m, 0.0) for s, m in zip(state, more))
        return shift + jnp.where(keep, totals(parts), 0.0), state

    zero = tuple(jnp.zeros((width, width), F32) for _ in range(kv))
    _, state = lax.fori_loop(0, slots, turn, (jnp.zeros((8, 1), F32), zero))
    finish(kv, queries, lin, grown, sparse, gain, state, out, buffer, sems)


def add_between(shift, i, far, sums):
    for j, total in sums:
        if j != i:
            shift = shift + jnp.where(far[j] < far[i], total, 0.0)
    return shift


def sparse_kernel(kv, n_column, per, distance, queries, biases, *refs):
    *pieces, out, states, shifts, scores = refs
    column = pieces[:n_column]
    tokens = per * BLK
    rep = queries.shape[1] // tokens
    far = distance()
    parts = [parts_of(p, kv) for p in pieces[1:]]
    suffix = suffixes([jnp.concatenate(p, axis=0) for p in zip(*parts)], tokens)
    sums = [(i, totals(p)) for i, p in enumerate(parts)]
    for i in range(len(far)):
        shift = add_between(jnp.zeros((8, 1), F32), i, far, sums)
        shifts[8 * i : 8 * i + 8, :] = jnp.broadcast_to(shift, (8, shifts.shape[1]))
    for i, piece in enumerate(pieces[1:]):
        for g, state in enumerate(own_states(kv, piece, suffix[:, 8 * i : 8 * i + 8], [0.0] * kv)):
            states[i * kv + g] = state
    for b in range(per):

        def own(i, shape):
            return iota(shape, 1) <= b * BLK + iota(shape, 0) // rep if i == 0 else None

        rows = [biases[b * n_column + i : b * n_column + i + 1, :] for i in range(n_column)]
        attend(kv, b, per, queries, column, rows, own, scores, out)


def last_kernel(kv, distance, queries, lin, grown, sparse, gain, states, shifts, *refs):
    *late, out, buffer, sems = refs
    far = distance()
    early = len(far) - len(late)
    tokens = out.shape[0]
    parts = [parts_of(p, kv) for p in late]
    suffix = suffixes([jnp.concatenate(p, axis=0) for p in zip(*parts)], tokens)
    sums = [(early + n, totals(p)) for n, p in enumerate(parts)]
    mine = [own_states(kv, p, suffix[:, 8 * n : 8 * n + 8], [0.0] * kv) for n, p in enumerate(late)]
    state = [0.0] * kv
    for i in range(len(far)):
        shift = add_between(shifts[8 * i : 8 * i + 8, :], i, far, sums)
        factor = jnp.where(far[i] < NEVER, jnp.exp(jnp.minimum(shift, 0.0)), 0.0)
        for g in range(kv):
            piece_state = states[i * kv + g] if i < early else mine[i - early][g]
            state[g] = state[g] + factor[g : g + 1, :] * piece_state
    finish(kv, queries, lin, grown, sparse, gain, state, out, buffer, sems)


def where_am_i():
    return lax.axis_index("seq"), lax.axis_index("inner")


def pick(table, at):
    value = jnp.int32(table[0])
    for n in range(1, len(table)):
        value = jnp.where(at == n, table[n], value)
    return value


def in_hbm(x):
    return pltpu.with_memory_space_constraint(x, pltpu.HBM)


def shards(queries, keys, values, log_decay, gain, block_list):
    tokens, heads, width = queries.shape
    kv = keys.shape[1]
    rows = tokens * (heads // kv)
    per = tokens // BLK
    n_seq, n_inner = lax.axis_size("seq"), lax.axis_size("inner")
    shape = jax.ShapeDtypeStruct

    def call(kernel, out_shape, in_specs, scratch, *args, cost=None, out_specs=None):
        one = not isinstance(out_shape, tuple)
        return pl.pallas_call(
            kernel,
            out_shape=out_shape,
            in_specs=in_specs,
            out_specs=out_specs or (VMEM if one else tuple(VMEM for _ in out_shape)),
            scratch_shapes=scratch,
            compiler_params=PARAMS,
            cost_estimate=cost,
        )(*args)

    piece = call(
        functools.partial(pack_kernel, kv),
        shape((2 * kv * tokens + EXTRA, width), BF16),
        [HBM] * 3,
        [
            pltpu.VMEM((2, kv * tokens, width), BF16),
            pltpu.VMEM((kv, tokens), F32),
            pltpu.VMEM((kv * tokens, width), F32),
            pltpu.SemaphoreType.DMA((3,)),
        ],
        in_hbm(keys.reshape(-1, width)),
        in_hbm(values.reshape(-1, width)),
        in_hbm(log_decay.T),
    )
    few = n_seq == 4 and n_inner == 2

    def numbers():
        z, x = where_am_i()
        found = [z * n_inner + x]
        for table in held:
            other = pick(table, z)
            found.append(jnp.where(other < z, other * n_inner + x, -1))
        return found

    def distance():
        z, x = where_am_i()
        mine, theirs = [], [jnp.where(x == 1, 1, NEVER)]
        for table in held:
            other = pick(table, z)
            mine.append(jnp.where(other < z, (z - other) * n_inner, NEVER))
            theirs.append(jnp.where(other < z, (z - other) * n_inner + jnp.where(x == 1, 1, -1), NEVER))
        return mine + theirs

    if few:
        first, second, third = (
            [(0, 2), (2, 3), (1, 1)],
            [(0, 1), (1, 3), (3, 2)],
            [(1, 2), (2, 3)],
        )
        came = [{b: a for a, b in pairs} for pairs in (first, second, third)]
        held = [
            [came[0].get(i, n_seq) for i in range(4)],
            [came[1].get(i, n_seq) for i in range(4)],
            [came[0].get(came[2].get(i, n_seq), n_seq) for i in range(4)],
        ]

    q, lin, grown, biases, gain = call(
        functools.partial(local_kernel, kv, numbers if few else None),
        (
            shape((kv, rows, width), BF16),
            shape((kv, rows, width), F32),
            shape((kv, rows, tokens), F32),
            shape((8, tokens), F32),
            shape(gain.shape, F32),
        ),
        [HBM, VMEM, SMEM, HBM],
        [pltpu.VMEM(queries.shape, BF16), pltpu.SemaphoreType.DMA((2,))],
        in_hbm(queries),
        piece,
        block_list,
        in_hbm(gain),
        cost=pl.CostEstimate(flops=4 * 10**9, bytes_accessed=4 * 10**6, transcendentals=10**6),
    )
    if few:

        def swap(x):
            return lax.ppermute(x, "inner", [(0, 1), (1, 0)])

        theirs = swap(piece)
        got1 = lax.ppermute(piece, "seq", first)
        got2 = lax.ppermute(piece, "seq", second)
        got1, q, theirs = lax.optimization_barrier((got1, q, theirs))
        theirs1 = swap(got1)
        got3 = lax.ppermute(got1, "seq", third)
        column = [piece, got1, got2, got3]
        other = [theirs, theirs1, swap(got2), swap(got3)]

    out_shape = shape((tokens, heads, width), BF16)
    write_out = [pltpu.VMEM(out_shape.shape, BF16), pltpu.SemaphoreType.DMA((GROUPS,))]
    if few:
        early = column[1:] + other[:N_EARLY]
        late = other[N_EARLY:]
        sparse, states, shifts = call(
            functools.partial(sparse_kernel, kv, n_seq, per, distance),
            (
                shape((kv, rows, width), F32),
                shape((len(early) * kv, width, width), F32),
                shape(((len(early) + len(late)) * 8, width), F32),
            ),
            [VMEM] * (3 + len(early)),
            [pltpu.VMEM((rows // per, n_seq * tokens), F32)],
            q,
            biases,
            piece,
            *early,
        )
        return call(
            functools.partial(last_kernel, kv, distance),
            out_shape,
            [VMEM] * (7 + len(late)),
            write_out,
            q,
            lin,
            grown,
            sparse,
            gain,
            states,
            shifts,
            *late,
            out_specs=HBM,
        )

    column = lax.all_gather(piece, "seq")
    everything = lax.all_gather(column, "inner").reshape(n_inner * n_seq, *piece.shape)

    def ids():
        z, x = where_am_i()
        return z * n_inner + x, lambda i: i * n_inner + x

    def place(n):
        z, x = where_am_i()
        p = n_seq * n_inner - 1 - n
        return lax.rem(p, n_inner) * n_seq + lax.div(p, n_inner), p < z * n_inner + x

    sparse = call(
        functools.partial(column_kernel, kv, n_seq, ids),
        shape((kv, rows, width), F32),
        [VMEM, SMEM, VMEM],
        [pltpu.VMEM((rows // per, n_seq * tokens), F32)],
        q,
        block_list,
        column,
    )
    return call(
        functools.partial(final_kernel, kv, n_seq * n_inner, place),
        out_shape,
        [VMEM] * 6,
        write_out,
        q,
        lin,
        grown,
        sparse,
        gain,
        everything,
        out_specs=HBM,
    )


def solution(mesh):
    tokens = P(("groups", "seq", "inner"), "head", None)
    return jax.shard_map(
        shards,
        mesh=mesh,
        in_specs=(
            tokens,
            tokens,
            tokens,
            P(("groups", "seq", "inner"), "head"),
            P("head", None),
            P(("groups", "seq", "inner"), None),
        ),
        out_specs=tokens,
        check_vma=False,
    )
```
